32 devices in a mesh: groups: 2 (over x), hyp: 8 (over z, y), tensor: 2 (over core).
Axes of the slice: x: 2, y: 2, z: 4, core: 2. Of those that a mesh axis runs over, the one named last changes fastest.
Arguments:
- queries: bfloat16 [2048, 8192], P(('groups', 'hyp'), 'tensor'), parts along dimension 0, may hold values from -48 to 48
- key_rows: bfloat16 [2048, 1024], P(('groups', 'hyp'), 'tensor'), parts along dimension 0, may hold values from -4 to 4
- value_rows: bfloat16 [2048, 1024], P(('groups', 'hyp'), 'tensor'), parts along dimension 0, may hold values from -6 to 6
- out_grad: bfloat16 [2048, 8192], P(('groups', 'hyp'), 'tensor'), parts along dimension 0, may hold values from -6 to 6
- token_parent: int32 [2048], P('groups'), parts along dimension 0, may hold values from -1 to 126, as said below
- block_parent: int32 [16], P('groups'), parts along dimension 0, may hold values from -1 to 7, as said below
Outputs:
- query_grad: bfloat16 [2048, 8192], P(('groups', 'hyp'), 'tensor'), parts along dimension 0
- key_grad: bfloat16 [2048, 1024], P(('groups', 'hyp'), 'tensor'), parts along dimension 0
- value_grad: bfloat16 [2048, 1024], P(('groups', 'hyp'), 'tensor'), parts along dimension 0
The draws below stay inside these ranges and needn't reach their ends.
There are 2 independent parts, one for each index of `groups`. The reference program is written for one: setup_inputs(seed, part) draws one part's arguments, and reference() takes and returns one part's arrays. A program takes and returns all parts, laid end to end along the dimension named above; each array names one. Nothing has to cross between parts.
Inputs may be any that keep to these rules, and one draw needn't show every extreme that they name: `token_parent`: each entry is -1 or an earlier position of the same block; the last position of every block has parent 128 - 2. `block_parent`: the 1 block of each run of 1 block (run r holds blocks r * 1 on) are all -1 or share one parent block that lies in another run; no block has more than 4 ancestor blocks, and some block has exactly 4.
All inputs are finite; a program needn't handle non-finite values.
Results may differ from the reference program's by a relative error of at most 0.009.
Values may be sent and summed in bfloat16 or wider, within the bound.
A program may use at most 128 MiB of HBM per device.

```python
import jax
import jax.numpy as jnp
from jax import lax

HQ = 64
HK = 8
HD = 128
BLOCK = 128
BLOCKS_DEV = 1
LEVELS = 4
BLOCKS = 8
TOKENS = 1024


def shared_keys(base_key):
    return jnp.clip(jax.random.normal(base_key, (TOKENS, HK * HD), jnp.float32), -4.0, 4.0)


def draw_key_rows(key, part):
    base_rows = shared_keys(key)
    return base_rows.astype(jnp.bfloat16)


def draw_queries(key, part):
    key = jax.random.fold_in(key, 13)
    drawn = jnp.clip(jax.random.normal(key, (TOKENS, HQ * HD), jnp.float32), -4.0, 4.0)
    return drawn.astype(jnp.bfloat16)


def draw_token_parent(key, part):
    key = jax.random.fold_in(key, 7)
    first_key, second_key = jax.random.split(key)
    positions = jnp.arange(TOKENS, dtype=jnp.int32) % BLOCK
    along = jax.random.randint(first_key, (TOKENS,), 0, 4) < 3
    jumped = jax.random.randint(second_key, (TOKENS,), -1, positions)
    parents = jnp.where(along, positions - 1, jumped)
    parents = jnp.where(positions == BLOCK - 1, BLOCK - 2, parents)
    return parents.astype(jnp.int32)


def draw_block_parent(key, part):
    key = jax.random.fold_in(key, 5)
    device_total = BLOCKS // BLOCKS_DEV
    order_key, roll_key, score_key, slot_key = jax.random.split(key, 4)
    ordering = jax.random.permutation(order_key, device_total).astype(jnp.int32)
    last_device = device_total - 1
    ordering = jnp.where(ordering == last_device, ordering[0], ordering)
    ordering = ordering.at[0].set(last_device).astype(jnp.int32)
    root_roll = jax.random.randint(roll_key, (device_total,), 0, 4)
    positions = jnp.arange(device_total, dtype=jnp.int32)
    scores = jax.random.randint(score_key, (device_total, device_total), 0, 65536) * device_total + positions[None, :]
    slot_pick = jax.random.randint(slot_key, (device_total,), 0, BLOCKS_DEV)
    slot_pick = slot_pick.at[1].set(BLOCKS_DEV - 1).astype(jnp.int32)

    def place(spot, state):
        depths, parent_spot = state
        eligible = (positions < spot) & (depths < LEVELS)
        chosen = jnp.argmax(jnp.where(eligible, scores[spot], -1)).astype(jnp.int32)
        chained = spot <= LEVELS
        choose = jnp.where(chained, spot - 1, chosen)
        is_root = (spot == 0) | ~chained & (root_roll[spot] == 0)
        choose = jnp.where(is_root, -1, choose).astype(jnp.int32)
        new_depth = jnp.where(is_root, 0, depths[jnp.maximum(choose, 0)] + 1)
        depths = depths.at[spot].set(new_depth.astype(jnp.int32))
        parent_spot = parent_spot.at[spot].set(choose)
        return (depths, parent_spot)
    start_state = (jnp.zeros((device_total,), jnp.int32), jnp.full((device_total,), -1, jnp.int32))
    depths, parent_spot = lax.fori_loop(0, device_total, place, start_state)
    parent_device = ordering[jnp.maximum(parent_spot, 0)]
    parent_block = jnp.where(parent_spot >= 0, parent_device * BLOCKS_DEV + slot_pick, -1).astype(jnp.int32)
    by_device = jnp.zeros((device_total,), jnp.int32).at[ordering].set(parent_block)
    return jnp.repeat(by_device, BLOCKS_DEV).astype(jnp.int32)


def block_levels(stream_key, shape, cuts, smallest, top_value):
    gain = 1.0
    for axis_at, parts in cuts:
        heights = jax.random.uniform(jax.random.fold_in(jax.random.fold_in(stream_key, 6), axis_at), (parts,), jnp.float32, smallest / len(cuts), top_value / len(cuts))
        gain = gain * jnp.repeat(jnp.exp(heights), shape[axis_at] // parts).reshape((-1,) + (1,) * (len(shape) - 1 - axis_at))
    return gain


def centred(key, dims, spread, reach, shards=(), held_as=jnp.bfloat16):
    values = jax.random.normal(key, dims, jnp.float32) * spread
    if len(shards) > 0:
        values = block_levels(key, dims, shards, -0.22, 0.18) * values
    return jnp.clip(values, min=-reach, max=reach).astype(held_as)


def setup_inputs(seed: int = 0, part: int = 0) -> dict:
    keys = jax.random.split(jax.random.key(seed), 7)
    part_splits = jax.random.split(jax.random.fold_in(keys[6], part), 7)
    queries = draw_queries(jax.random.fold_in(jax.random.fold_in(keys[6], part), 71), part)
    key_rows = draw_key_rows(jax.random.fold_in(jax.random.fold_in(keys[6], part), 71), part)
    value_rows = centred(part_splits[2], (TOKENS, HK * HD), 1.0, 6.0, ((0, 8), (1, 2)))
    out_grad = centred(part_splits[3], (TOKENS, HQ * HD), 1.0, 6.0, ((0, 8), (1, 2)))
    token_parent = draw_token_parent(jax.random.fold_in(jax.random.fold_in(keys[6], part), 71), part)
    block_parent = draw_block_parent(jax.random.fold_in(jax.random.fold_in(keys[6], part), 71), part)
    return {"queries": queries, "key_rows": key_rows, "value_rows": value_rows, "out_grad": out_grad, "token_parent": token_parent, "block_parent": block_parent}


def rounded(values_in):
    lowered = lax.optimization_barrier(values_in.astype(jnp.bfloat16))
    return lowered.astype(jnp.float32)


def closure(parents):
    block_len = parents.shape[1]
    positions = jnp.arange(block_len, dtype=jnp.int32)
    direct = parents[:, :, None] == positions[None, None, :]
    itself = (positions[:, None] == positions[None, :])[None]
    reach_set = (direct | itself).astype(jnp.float32)
    for sweep in range((block_len - 1).bit_length()):
        reach_set = jnp.minimum(jnp.einsum('mij,mjk->mik', reach_set, reach_set), 1.0)
    return reach_set > 0.5


def device_ancestors(block_parent, per_dev):
    current = block_parent[::per_dev]
    levels = []
    for level in range(LEVELS):
        levels.append(current)
        current = jnp.where(current >= 0, block_parent[jnp.maximum(current, 0)], -1)
    return jnp.stack(levels, 1).astype(jnp.int32)


def reference(queries, key_rows, value_rows, out_grad, token_parent, block_parent):
    device_total = BLOCKS // BLOCKS_DEV
    local_rows = BLOCKS_DEV * BLOCK
    ratio = HQ // HK
    softmax_scale = HD ** -0.5
    ancestor_table = device_ancestors(block_parent, BLOCKS_DEV)
    parents_by_block = token_parent.reshape(BLOCKS, BLOCK)
    key_blocks = key_rows.reshape(BLOCKS, BLOCK, HK, HD)
    value_blocks = value_rows.reshape(BLOCKS, BLOCK, HK, HD)

    def device_step(accumulators, device_number):
        key_accum, value_accum = accumulators
        first_row = device_number * local_rows
        local_query_rows = lax.dynamic_slice_in_dim(queries, first_row, local_rows, 0)
        local_query_rows = local_query_rows.astype(jnp.float32).reshape(BLOCKS_DEV, BLOCK, HK, ratio, HD)
        local_gradient_rows = lax.dynamic_slice_in_dim(out_grad, first_row, local_rows, 0)
        local_gradient_rows = local_gradient_rows.astype(jnp.float32).reshape(BLOCKS_DEV, BLOCK, HK, ratio, HD)
        own_ids = (device_number * BLOCKS_DEV + jnp.arange(BLOCKS_DEV, dtype=jnp.int32)).astype(jnp.int32)
        own_key_rows = key_blocks[own_ids].astype(jnp.float32)
        own_value_rows = value_blocks[own_ids].astype(jnp.float32)
        my_ancestors = ancestor_table[device_number]
        is_valid = my_ancestors >= 0
        safe_ids = jnp.maximum(my_ancestors, 0).astype(jnp.int32)
        key_anc = key_blocks[safe_ids].astype(jnp.float32)
        value_anc = value_blocks[safe_ids].astype(jnp.float32)
        spine_mask = closure(parents_by_block[safe_ids])[:, BLOCK - 1, :] & is_valid[:, None]
        own_mask = closure(parents_by_block[own_ids])
        score_anc = jnp.einsum('bqgrd,lkgd->bgrqlk', local_query_rows, key_anc) * softmax_scale
        score_own = jnp.einsum('bqgrd,bkgd->bgrqk', local_query_rows, own_key_rows) * softmax_scale
        score_anc = jnp.where(spine_mask, score_anc, -jnp.inf)
        score_own = jnp.where(own_mask[:, None, None], score_own, -jnp.inf)
        row_max = jnp.maximum(jnp.max(score_anc, axis=(4, 5)), jnp.max(score_own, axis=4))
        exp_anc = jnp.exp(score_anc - row_max[..., None, None])
        exp_own = jnp.exp(score_own - row_max[..., None])
        row_sum = jnp.sum(exp_anc, axis=(4, 5)) + jnp.sum(exp_own, axis=4)
        prob_anc = exp_anc / row_sum[..., None, None]
        prob_own = exp_own / row_sum[..., None]
        dprob_anc = jnp.einsum('bqgrd,lkgd->bgrqlk', local_gradient_rows, value_anc)
        dprob_own = jnp.einsum('bqgrd,bkgd->bgrqk', local_gradient_rows, own_value_rows)
        delta_row = jnp.sum(prob_anc * dprob_anc, axis=(4, 5)) + jnp.sum(prob_own * dprob_own, axis=4)
        dscore_anc = rounded(prob_anc * (dprob_anc - delta_row[..., None, None]))
        own_score_gradient = rounded(prob_own * (dprob_own - delta_row[..., None]))
        plow_anc = rounded(prob_anc)
        own_probs_reduced = rounded(prob_own)
        query_part = softmax_scale * (jnp.einsum('bgrqlk,lkgd->bqgrd', dscore_anc, key_anc)
                                      + jnp.einsum('bgrqk,bkgd->bqgrd', own_score_gradient, own_key_rows))
        query_part = query_part.astype(jnp.bfloat16).reshape(local_rows, HQ * HD)
        keyg_anc = rounded(softmax_scale * jnp.einsum('bgrqlk,bqgrd->lkgd', dscore_anc, local_query_rows))
        valg_anc = rounded(jnp.einsum('bgrqlk,bqgrd->lkgd', plow_anc, local_gradient_rows))
        keyg_own = rounded(softmax_scale * jnp.einsum('bgrqk,bqgrd->bkgd', own_score_gradient, local_query_rows))
        own_value_gradient = rounded(jnp.einsum('bgrqk,bqgrd->bkgd', own_probs_reduced, local_gradient_rows))
        level_keep = is_valid[:, None, None, None]
        key_accum = key_accum.at[safe_ids].add(jnp.where(level_keep, keyg_anc, 0.0))
        value_accum = value_accum.at[safe_ids].add(jnp.where(level_keep, valg_anc, 0.0))
        key_accum = key_accum.at[own_ids].add(keyg_own)
        value_accum = value_accum.at[own_ids].add(own_value_gradient)
        return (key_accum, value_accum), query_part

    empty = jnp.zeros((BLOCKS, BLOCK, HK, HD), jnp.float32)
    sums_out, query_parts = lax.scan(device_step, (empty, empty), jnp.arange(device_total, dtype=jnp.int32))
    query_grad = query_parts.reshape(TOKENS, HQ * HD)
    key_grad = sums_out[0].reshape(TOKENS, HK * HD).astype(jnp.bfloat16)
    value_grad = sums_out[1].reshape(TOKENS, HK * HD).astype(jnp.bfloat16)
    return (query_grad, key_grad, value_grad)
```

```python
import functools

import jax
import jax.numpy as jnp
from jax import lax
from jax.experimental import pallas as pl
from jax.experimental.pallas import tpu as pltpu
from jax.sharding import PartitionSpec as P

HD = 128
BLOCK = 128
MESH = pl.DeviceIdType.MESH
CHUNK_HEADS = 2
MASKED = -1e30


def dot(a, b, dims):
    return lax.dot_general(a, b, (dims, ((), ())), preferred_element_type=jnp.float32)


def closure_transposed(parents):
    rows = lax.broadcasted_iota(jnp.int32, (BLOCK, BLOCK), 0)
    cols = lax.broadcasted_iota(jnp.int32, (BLOCK, BLOCK), 1)
    hit = (parents == rows) | (rows == cols)
    return jnp.where(hit, 1.0, 0.0).astype(jnp.bfloat16)


def kernel(Z, Y, G, R, L, *refs):
    bp_ref, tp_ref, q_ref, do_ref, k_ref, v_ref, dq_ref, dk_ref, dv_ref = refs[:9]
    refs = refs[9:]
    kv = refs[:G]
    part = refs[G:2 * G]
    ysend = refs[2 * G:3 * G]
    yrecv = refs[3 * G:4 * G]
    zsend = refs[4 * G:5 * G]
    zrecv = refs[5 * G:6 * G]
    (cur, kt, bias, acc_k, acc_v, own_sum,
     agz_s, agz_r, agy_s, agy_r, rsy_s, rsy_r, rsz_s, rsz_r) = refs[6 * G:]
    scale = HD ** -0.5
    me = lax.axis_index("hyp")
    z, y = me // Y, me % Y
    partner = z * Y + (Y - 1 - y)
    column = [((z + k) % Z) * Y + y for k in range(Z)]
    source = [((z + Z - k) % Z) * Y + y for k in range(Z)]

    barrier = pltpu.get_barrier_semaphore()
    for k in range(1, Z):
        pl.semaphore_signal(barrier, inc=1, device_id={"hyp": column[k]}, device_id_type=MESH)
    if Y > 1:
        pl.semaphore_signal(barrier, inc=1, device_id={"hyp": partner}, device_id_type=MESH)
    pl.semaphore_wait(barrier, Z - 1 + (Y - 1))

    def push(src, dst, s_sem, r_sem, target):
        return pltpu.make_async_remote_copy(
            src_ref=src, dst_ref=dst, send_sem=s_sem, recv_sem=r_sem,
            device_id={"hyp": target}, device_id_type=MESH)

    agz, agy = {}, {}
    for g in range(G):
        cols = slice(g * HD, (g + 1) * HD)
        kv[g][me, :, :HD] = k_ref[:, cols]
        kv[g][me, :, HD:] = v_ref[:, cols]
        for k in range(1, Z):
            agz[g, k] = push(kv[g].at[me], kv[g].at[me], agz_s.at[g, k], agz_r.at[g, k], column[k])
            agz[g, k].start()
        if Y > 1:
            agy[g, 0] = push(kv[g].at[me], kv[g].at[me], agy_s.at[g, 0], agy_r.at[g, 0], partner)
            agy[g, 0].start()

    def forward(g):
        for k in range(1, Z):
            agz[g, k].wait_recv()
            if Y > 1:
                slot = kv[g].at[source[k]]
                agy[g, k] = push(slot, slot, agy_s.at[g, k], agy_r.at[g, k], partner)
                agy[g, k].start()

    def parent_of(a):
        return jnp.where(a >= 0, bp_ref[jnp.maximum(a, 0)], -1)

    ancestors = [bp_ref[me]]
    for l in range(1, L):
        ancestors.append(parent_of(ancestors[-1]))
    safe = [jnp.maximum(a, 0) for a in ancestors]
    reach = [closure_transposed(tp_ref[b]) for b in safe + [me]]
    for sweep in range((BLOCK - 1).bit_length()):
        reach = [jnp.minimum(dot(r, r, ((1,), (0,))), 1.0).astype(jnp.bfloat16) for r in reach]
    for l in range(L):
        spine = reach[l][:, BLOCK - 1:].astype(jnp.float32) * jnp.where(ancestors[l] >= 0, 1.0, 0.0)
        spine = jnp.broadcast_to(spine, (BLOCK, HD))
        bias[pl.ds(l * BLOCK, BLOCK), :] = jnp.where(spine > 0.5, 0.0, MASKED)
    bias[pl.ds(L * BLOCK, BLOCK), :] = jnp.where(reach[L].astype(jnp.float32) > 0.5, 0.0, MASKED)

    def level_of(block):
        slot = jnp.where(block == me, L, L + 1)
        for l in range(L):
            slot = jnp.where(ancestors[l] == block, l, slot)
        return slot

    def compute(g):
        for l in range(L):
            cur[pl.ds(l * BLOCK, BLOCK), :] = kv[g][safe[l]]
        cur[pl.ds(L * BLOCK, BLOCK), :] = kv[g][me]
        kt[...] = cur[:, :HD].T
        acc_k[...] = jnp.zeros_like(acc_k)
        acc_v[...] = jnp.zeros_like(acc_v)

        @pl.loop(0, R // CHUNK_HEADS)
        def _(c):
            at = [pl.ds(pl.multiple_of((g * R + c * CHUNK_HEADS + h) * HD, HD), HD)
                  for h in range(CHUNK_HEADS)]
            qc = jnp.concatenate([q_ref[:, a] for a in at], 0)
            dc = jnp.concatenate([do_ref[:, a] for a in at], 0)
            keys, values = cur[:, :HD], cur[:, HD:]
            mask = jnp.concatenate([bias[...]] * CHUNK_HEADS, 1)
            s = dot(keys, qc, ((1,), (1,))) * scale + mask
            dp = dot(values, dc, ((1,), (1,)))
            e = jnp.exp(s - jnp.max(s, 0, keepdims=True))
            inv = 1.0 / jnp.sum(e, 0, keepdims=True)
            p = e * inv
            delta = jnp.sum(p * dp, 0, keepdims=True)
            ds = (p * (dp - delta)).astype(jnp.bfloat16)
            plow = p.astype(jnp.bfloat16)
            dqt = (dot(kt[...], ds, ((1,), (0,))) * scale).T
            for h in range(CHUNK_HEADS):
                dq_ref[:, at[h]] = dqt[h * BLOCK:(h + 1) * BLOCK].astype(jnp.bfloat16)
            acc_k[...] += dot(ds, qc, ((1,), (0,)))
            acc_v[...] += dot(plow, dc, ((1,), (0,)))

        for l in range(L + 1):
            rows = pl.ds(l * BLOCK, BLOCK)
            part[g][l, :, :HD] = (acc_k[rows, :] * scale).astype(jnp.bfloat16)
            part[g][l, :, HD:] = acc_v[rows, :].astype(jnp.bfloat16)
        part[g][L + 1] = jnp.zeros((BLOCK, 2 * HD), jnp.bfloat16)

    rsy, rsz = {}, {}

    def scatter_y(g):
        if Y > 1:
            for zt in range(Z):
                ysend[g][zt] = part[g][level_of(zt * Y + (Y - 1 - y))]
            rsy[g] = push(ysend[g], yrecv[g], rsy_s.at[g], rsy_r.at[g], partner)
            rsy[g].start()

    def scatter_z(g):
        if Y > 1:
            rsy[g].wait_recv()
        for k in list(range(1, Z)) + [0]:
            zt = (z + k) % Z
            total = part[g][level_of(column[k])].astype(jnp.float32)
            if Y > 1:
                total = total + yrecv[g][zt].astype(jnp.float32)
            if k == 0:
                own_sum[g] = total
            else:
                zsend[g][k - 1] = total.astype(jnp.bfloat16)
                rsz[g, k] = push(zsend[g].at[k - 1], zrecv[g].at[k - 1],
                                 rsz_s.at[g, k], rsz_r.at[g, k], column[k])
                rsz[g, k].start()

    def finish(g):
        total = own_sum[g]
        for k in range(1, Z):
            rsz[g, k].wait_recv()
            total = total + zrecv[g][k - 1].astype(jnp.float32)
        cols = slice(g * HD, (g + 1) * HD)
        dk_ref[:, cols] = total[:, :HD].astype(jnp.bfloat16)
        dv_ref[:, cols] = total[:, HD:].astype(jnp.bfloat16)

    forward(0)
    for g in range(G):
        if g + 1 < G:
            forward(g + 1)
        if Y > 1:
            for k in range(Z):
                agy[g, k].wait_recv()
        compute(g)
        scatter_y(g)
        if g > 0:
            scatter_z(g - 1)
    scatter_z(G - 1)
    for g in range(G):
        finish(g)
    for copy in list(agz.values()) + list(agy.values()) + list(rsy.values()) + list(rsz.values()):
        copy.wait_send()


def on_device(queries, key_rows, value_rows, out_grad, token_parent, block_parent):
    H = lax.axis_size("hyp")
    Y = 2 if H == 8 else 1
    Z = H // Y
    L = min(5, H - 4)
    G = key_rows.shape[1] // HD
    R = queries.shape[1] // key_rows.shape[1]
    keys = (L + 1) * BLOCK
    bf, f32 = jnp.bfloat16, jnp.float32
    vmem = pl.BlockSpec(memory_space=pltpu.VMEM)
    dma = pltpu.SemaphoreType.DMA
    scratch = (
        [pltpu.VMEM((H, BLOCK, 2 * HD), bf)] * G
        + [pltpu.VMEM((L + 2, BLOCK, 2 * HD), bf)] * G
        + [pltpu.VMEM((Z, BLOCK, 2 * HD), bf)] * (2 * G)
        + [pltpu.VMEM((Z - 1, BLOCK, 2 * HD), bf)] * (2 * G)
        + [
            pltpu.VMEM((keys, 2 * HD), bf),
            pltpu.VMEM((HD, keys), bf),
            pltpu.VMEM((keys, HD), f32),
            pltpu.VMEM((keys, HD), f32),
            pltpu.VMEM((keys, HD), f32),
            pltpu.VMEM((G, BLOCK, 2 * HD), f32),
        ]
        + [dma((G, Z))] * 4
        + [dma((G,))] * 2
        + [dma((G, Z))] * 2
    )
    return pl.pallas_call(
        functools.partial(kernel, Z, Y, G, R, L),
        out_shape=(
            jax.ShapeDtypeStruct(queries.shape, bf),
            jax.ShapeDtypeStruct(key_rows.shape, bf),
            jax.ShapeDtypeStruct(value_rows.shape, bf),
        ),
        in_specs=[pl.BlockSpec(memory_space=pltpu.SMEM)] + [vmem] * 5,
        out_specs=(vmem, vmem, vmem),
        scratch_shapes=scratch,
        compiler_params=pltpu.CompilerParams(
            collective_id=0, has_side_effects=True, vmem_limit_bytes=48 * 1024 * 1024),
        name="tree_attention_backward",
    )(block_parent, token_parent.reshape(-1, 1, BLOCK), queries, out_grad, key_rows, value_rows)


def solution(mesh):
    rows = P(("groups", "hyp"), "tensor")
    return jax.shard_map(
        on_device, mesh=mesh,
        in_specs=(rows, rows, rows, rows, P("groups"), P("groups")),
        out_specs=(rows, rows, rows), check_vma=False)
```

```python
import functools

import jax
import jax.numpy as jnp
from jax import lax
from jax.experimental import pallas as pl
from jax.experimental.pallas import tpu as pltpu
from jax.sharding import PartitionSpec as P

HD = 128
BLOCK = 128
MESH = pl.DeviceIdType.MESH
CHUNK_HEADS = 4
GATHER_PAIRS = (3,)
MASKED = -1e30


def dot(a, b, dims):
    return lax.dot_general(a, b, (dims, ((), ())), preferred_element_type=jnp.float32)


def closure_transposed(parents):
    rows = lax.broadcasted_iota(jnp.int32, (BLOCK, BLOCK), 0)
    cols = lax.broadcasted_iota(jnp.int32, (BLOCK, BLOCK), 1)
    hit = (parents == rows) | (rows == cols)
    return jnp.where(hit, 1.0, 0.0).astype(jnp.bfloat16)


def kernel(Z, Y, G, R, L, gather_pairs, *refs):
    (bp_ref, tp_hbm, q_hbm, do_hbm, k_hbm, v_hbm, dq_ref, dk_ref, dv_ref) = refs[:9]
    refs = refs[9:]
    kv, part, ysend, yrecv, zsend, zrecv = (refs[i * G:(i + 1) * G] for i in range(6))
    (tp_ref, q_ref, do_ref, cur, kt, bias, acc_k, acc_v, own_sum, in_sem,
     agu_s, agu_r, agd_s, agd_r, agy_s, agy_r,
     rsy_s, rsy_r, rsz_s, rsz_r) = refs[6 * G:]
    scale = HD ** -0.5
    me = lax.axis_index("hyp")
    z, y = me // Y, me % Y
    partner = z * Y + (Y - 1 - y)
    below, above = me - Y, me + Y
    has_below, has_above = z > 0, z < Z - 1

    loads = []

    def load(src, dst):
        copy = pltpu.make_async_copy(src, dst, in_sem.at[len(loads)])
        copy.start()
        loads.append(copy)

    for g in range(G):
        cols = pl.ds(g * HD, HD)
        load(k_hbm.at[:, cols], kv[g].at[me, :, pl.ds(0, HD)])
        load(v_hbm.at[:, cols], kv[g].at[me, :, pl.ds(HD, HD)])
    load(tp_hbm, tp_ref)
    load(q_hbm, q_ref)
    load(do_hbm, do_ref)

    barrier = pltpu.get_barrier_semaphore()

    for k in range(1, Z):
        pl.semaphore_signal(
            barrier, inc=1, device_id={"hyp": lax.rem(z + k, Z) * Y + y}, device_id_type=MESH)
    if Y > 1:
        pl.semaphore_signal(barrier, inc=1, device_id={"hyp": partner}, device_id_type=MESH)
    pl.semaphore_wait(barrier, Z - 1 + Y - 1)

    sent = []

    class Push:
        def __init__(self, src, dst, s_sem, r_sem, target):
            self.make = lambda: pltpu.make_async_remote_copy(
                src_ref=src, dst_ref=dst, send_sem=s_sem, recv_sem=r_sem,
                device_id={"hyp": target}, device_id_type=MESH)

        def start(self, cond=None):
            sent.append((cond, self))
            if cond is None:
                self.make().start()
            else:
                pl.when(cond)(lambda: self.make().start())

        def wait_recv(self, cond=None):
            if cond is None:
                self.make().wait_recv()
            else:
                pl.when(cond)(lambda: self.make().wait_recv())

    def slot(g, zs):
        zs = jnp.minimum(jnp.maximum(zs, 0), Z - 1)
        if g in gather_pairs:
            return kv[g].at[pl.ds(zs * Y, Y)]
        return kv[g].at[zs * Y + y]

    def gather_up(g, k):
        item = slot(g, z - k)
        return Push(item, item, agu_s.at[g, k], agu_r.at[g, k + 1], above)

    def gather_down(g, k):
        item = slot(g, z + k)
        return Push(item, item, agd_s.at[g, k], agd_r.at[g, k + 1], below)

    def gather_across(g, k, zs):
        item = kv[g].at[jnp.minimum(jnp.maximum(zs, 0), Z - 1) * Y + y]
        return Push(item, item, agy_s.at[g, k], agy_r.at[g, k], partner)

    def gather_step(g, k):
        if k == 0:
            if g in gather_pairs and Y > 1:
                gather_across(g, 0, z).wait_recv()
            gather_up(g, 0).start(has_above)
            gather_down(g, 0).start(has_below)
            return
        up_here, down_here = z >= k, z + k < Z
        Push(slot(g, z - k), slot(g, z - k), agu_s.at[g, k], agu_r.at[g, k], me).wait_recv(up_here)
        if k < Z - 1:
            gather_up(g, k).start(up_here & has_above)
        if g not in gather_pairs and Y > 1:
            gather_across(g, k, z - k).start(up_here)
        Push(slot(g, z + k), slot(g, z + k), agd_s.at[g, k], agd_r.at[g, k], me).wait_recv(down_here)
        if k < Z - 1:
            gather_down(g, k).start(down_here & has_below)
        if g not in gather_pairs and Y > 1:
            gather_across(g, Z + k, z + k).start(down_here)

    def gather_done(g):
        if g in gather_pairs or Y == 1:
            return
        gather_across(g, 0, z).wait_recv()
        for k in range(1, Z):
            gather_across(g, k, z - k).wait_recv(z >= k)
            gather_across(g, Z + k, z + k).wait_recv(z + k < Z)

    def parent_of(a):
        return jnp.where(a >= 0, bp_ref[jnp.maximum(a, 0)], -1)

    ancestors = [bp_ref[me]]
    for l in range(1, L):
        ancestors.append(parent_of(ancestors[-1]))
    safe = [jnp.maximum(a, 0) for a in ancestors]

    def masks():
        reach = [closure_transposed(tp_ref[b]) for b in safe + [me]]
        for sweep in range((BLOCK - 1).bit_length()):
            reach = [jnp.minimum(dot(r, r, ((1,), (0,))), 1.0).astype(jnp.bfloat16) for r in reach]
        for l in range(L):
            spine = reach[l][:, BLOCK - 1:].astype(jnp.float32)
            spine = spine * jnp.where(ancestors[l] >= 0, 1.0, 0.0)
            spine = jnp.broadcast_to(spine, (BLOCK, HD))
            bias[pl.ds(l * BLOCK, BLOCK), :] = jnp.where(spine > 0.5, 0.0, MASKED)
        bias[pl.ds(L * BLOCK, BLOCK), :] = jnp.where(reach[L].astype(jnp.float32) > 0.5, 0.0, MASKED)

    def level_of(block):
        level = jnp.where(block == me, L, L + 1)
        for l in range(L):
            level = jnp.where(ancestors[l] == block, l, level)
        return level

    def compute_begin(g):
        for l in range(L):
            cur[pl.ds(l * BLOCK, BLOCK), :] = kv[g][safe[l]]
        cur[pl.ds(L * BLOCK, BLOCK), :] = kv[g][me]
        kt[...] = cur[:, :HD].T

    def compute_chunk(g, c):
        at = [pl.ds((g * R + c * CHUNK_HEADS + h) * HD, HD) for h in range(CHUNK_HEADS)]
        qc = jnp.concatenate([q_ref[:, a] for a in at], 0)
        dc = jnp.concatenate([do_ref[:, a] for a in at], 0)
        keys, values = cur[:, :HD], cur[:, HD:]
        mask = jnp.concatenate([bias[...]] * CHUNK_HEADS, 1)
        s = dot(keys, qc, ((1,), (1,))) * scale + mask
        dp = dot(values, dc, ((1,), (1,)))
        e = jnp.exp(s - jnp.max(s, 0, keepdims=True))
        inv = 1.0 / jnp.sum(e, 0, keepdims=True)
        p = e * inv
        delta = jnp.sum(p * dp, 0, keepdims=True)
        ds = (p * (dp - delta)).astype(jnp.bfloat16)
        plow = p.astype(jnp.bfloat16)
        dqt = (dot(kt[...], ds, ((1,), (0,))) * scale).T
        for h in range(CHUNK_HEADS):
            dq_ref[:, at[h]] = dqt[h * BLOCK:(h + 1) * BLOCK].astype(jnp.bfloat16)
        more_k, more_v = dot(ds, qc, ((1,), (0,))), dot(plow, dc, ((1,), (0,)))
        if c == 0:
            acc_k[...] = more_k
            acc_v[...] = more_v
        else:
            acc_k[...] += more_k
            acc_v[...] += more_v

    def compute_end(g):
        for l in range(L + 1):
            rows = pl.ds(l * BLOCK, BLOCK)
            part[g][l, :, :HD] = (acc_k[rows, :] * scale).astype(jnp.bfloat16)
            part[g][l, :, HD:] = acc_v[rows, :].astype(jnp.bfloat16)
        part[g][L + 1] = jnp.zeros((BLOCK, 2 * HD), jnp.bfloat16)

    column = [lax.rem(z + k, Z) * Y + y for k in range(Z)]

    def across(g, k):
        return Push(ysend[g].at[k], yrecv[g].at[k], rsy_s.at[g, k], rsy_r.at[g, k], partner)

    def along(g, k):
        return Push(zsend[g].at[k], zrecv[g].at[k], rsz_s.at[g, k], rsz_r.at[g, k], column[k])

    hops = list(range(1, Z)) + [0]

    def scatter_y(g):
        if Y > 1:
            for k in hops:
                ysend[g][k] = part[g][level_of(column[k] + (Y - 1 - y) - y)]
                across(g, k).start()

    def scatter_z(g):
        for k in hops:
            total = part[g][level_of(column[k])].astype(jnp.float32)
            if Y > 1:
                across(g, k).wait_recv()
                total = total + yrecv[g][k].astype(jnp.float32)
            if k == 0:
                own_sum[g] = total
            else:
                zsend[g][k] = total.astype(jnp.bfloat16)
                along(g, k).start()

    def finish(g):
        total = own_sum[g]
        for k in range(1, Z):
            along(g, k).wait_recv()
            total = total + zrecv[g][k].astype(jnp.float32)
        cols = slice(g * HD, (g + 1) * HD)
        dk_ref[:, cols] = total[:, :HD].astype(jnp.bfloat16)
        dv_ref[:, cols] = total[:, HD:].astype(jnp.bfloat16)

    for g in range(G):
        loads[2 * g].wait()
        loads[2 * g + 1].wait()
        if Y > 1:
            gather_across(g, 0, z).start()
        if g not in gather_pairs:
            gather_step(g, 0)
    for copy in loads[2 * G:]:
        copy.wait()
    masks()

    steps = [(g, k) for t in range(G + Z) for g in range(G) for k in [t - g] if 0 <= k < Z]
    steps = [(g, k) for g, k in steps if k > 0 or g in gather_pairs]

    def gather_until(g, k):
        while steps and (g, k) in steps:
            gather_step(*steps.pop(0))

    chunks = R // CHUNK_HEADS
    for g in range(G):
        gather_until(g, Z - 1)
        gather_done(g)
        compute_begin(g)
        for c in range(chunks):
            compute_chunk(g, c)
            if g + 1 < G:
                gather_until(g + 1, (Z - 1) * (c + 1) // chunks)
        compute_end(g)
        scatter_y(g)
        if g > 0:
            scatter_z(g - 1)
    scatter_z(G - 1)
    for g in range(G):
        finish(g)
    for cond, copy in sent:
        if cond is None:
            copy.make().wait_send()
        else:
            pl.when(cond)(lambda copy=copy: copy.make().wait_send())


def on_device(queries, key_rows, value_rows, out_grad, token_parent, block_parent):
    H = lax.axis_size("hyp")
    Y = 2 if H == 8 else 1
    Z = H // Y
    L = min(5, H - 4)
    G = key_rows.shape[1] // HD
    R = queries.shape[1] // key_rows.shape[1]
    keys = (L + 1) * BLOCK
    bf, f32 = jnp.bfloat16, jnp.float32
    vmem = pl.BlockSpec(memory_space=pltpu.VMEM)
    hbm = pl.BlockSpec(memory_space=pl.ANY)
    dma = pltpu.SemaphoreType.DMA
    tile = (BLOCK, 2 * HD)
    gather_pairs = GATHER_PAIRS if Y > 1 else tuple(range(G))
    scratch = (
        [pltpu.VMEM((H,) + tile, bf)] * G
        + [pltpu.VMEM((L + 2,) + tile, bf)] * G
        + [pltpu.VMEM((Z,) + tile, bf)] * (4 * G)
        + [
            pltpu.VMEM((token_parent.shape[0] // BLOCK, 1, BLOCK), jnp.int32),
            pltpu.VMEM(queries.shape, bf),
            pltpu.VMEM(out_grad.shape, bf),
            pltpu.VMEM((keys, 2 * HD), bf),
            pltpu.VMEM((HD, keys), bf),
            pltpu.VMEM((keys, HD), f32),
            pltpu.VMEM((keys, HD), f32),
            pltpu.VMEM((keys, HD), f32),
            pltpu.VMEM((G,) + tile, f32),
            dma((2 * G + 3,)),
        ]
        + [dma((G, Z))] * 4
        + [dma((G, 2 * Z))] * 2
        + [dma((G, Z))] * 4
    )
    return pl.pallas_call(
        functools.partial(kernel, Z, Y, G, R, L, gather_pairs),
        out_shape=(
            jax.ShapeDtypeStruct(queries.shape, bf),
            jax.ShapeDtypeStruct(key_rows.shape, bf),
            jax.ShapeDtypeStruct(value_rows.shape, bf),
        ),
        in_specs=[pl.BlockSpec(memory_space=pltpu.SMEM)] + [hbm] * 5,
        out_specs=(vmem, vmem, vmem),
        scratch_shapes=scratch,
        compiler_params=pltpu.CompilerParams(
            collective_id=0, has_side_effects=True, vmem_limit_bytes=56 * 1024 * 1024),
        name="tree_attention_backward",
    )(block_parent, token_parent.reshape(-1, 1, BLOCK), queries, out_grad, key_rows, value_rows)


def solution(mesh):
    rows = P(("groups", "hyp"), "tensor")
    return jax.shard_map(
        on_device, mesh=mesh,
        in_specs=(rows, rows, rows, rows, P("groups"), P("groups")),
        out_specs=(rows, rows, rows), check_vma=False)
```

```python
import functools

import jax
import jax.numpy as jnp
from jax import lax
from jax.experimental import pallas as pl
from jax.experimental.pallas import tpu as pltpu
from jax.sharding import PartitionSpec as P

HD = 128
BLOCK = 128
MESH = pl.DeviceIdType.MESH
CHUNK_HEADS = 4
GATHER_PAIRS = (3,)
AHEAD = 2
MASKED = -1e30


def dot(a, b, dims):
    return lax.dot_general(a, b, (dims, ((), ())), preferred_element_type=jnp.float32)


def closure_transposed(parents):
    rows = lax.broadcasted_iota(jnp.int32, (BLOCK, BLOCK), 0)
    cols = lax.broadcasted_iota(jnp.int32, (BLOCK, BLOCK), 1)
    hit = (parents == rows) | (rows == cols)
    return jnp.where(hit, 1.0, 0.0).astype(jnp.bfloat16)


def kernel(Z, Y, G, R, L, gather_pairs, *refs):
    (bp_ref, tp_hbm, q_hbm, do_hbm, k_hbm, v_hbm, dq_ref, dk_ref, dv_ref) = refs[:9]
    refs = refs[9:]
    kv, part, ysend, yrecv, zsend, zrecv = (refs[i * G:(i + 1) * G] for i in range(6))
    (tp_ref, q_ref, do_ref, cur, kt, bias, acc_k, acc_v, own_sum, in_sem,
     agu_s, agu_r, agd_s, agd_r, agy_s, agy_r,
     rsy_s, rsy_r, rsz_s, rsz_r) = refs[6 * G:]
    scale = HD ** -0.5
    me = lax.axis_index("hyp")
    z, y = me // Y, me % Y
    partner = z * Y + (Y - 1 - y)
    below, above = me - Y, me + Y
    has_below, has_above = z > 0, z < Z - 1

    loads = []

    def load(src, dst):
        copy = pltpu.make_async_copy(src, dst, in_sem.at[len(loads)])
        copy.start()
        loads.append(copy)

    for g in range(G):
        cols = pl.ds(g * HD, HD)
        load(k_hbm.at[:, cols], kv[g].at[me, :, pl.ds(0, HD)])
        load(v_hbm.at[:, cols], kv[g].at[me, :, pl.ds(HD, HD)])
    load(tp_hbm, tp_ref)
    load(q_hbm, q_ref)
    load(do_hbm, do_ref)

    barrier = pltpu.get_barrier_semaphore()

    for k in range(1, Z):
        pl.semaphore_signal(
            barrier, inc=1, device_id={"hyp": lax.rem(z + k, Z) * Y + y}, device_id_type=MESH)
    if Y > 1:
        pl.semaphore_signal(barrier, inc=1, device_id={"hyp": partner}, device_id_type=MESH)
    pl.semaphore_wait(barrier, Z - 1 + Y - 1)

    sent = []

    class Push:
        def __init__(self, src, dst, s_sem, r_sem, target):
            self.make = lambda: pltpu.make_async_remote_copy(
                src_ref=src, dst_ref=dst, send_sem=s_sem, recv_sem=r_sem,
                device_id={"hyp": target}, device_id_type=MESH)

        def start(self, cond=None):
            sent.append((cond, self))
            if cond is None:
                self.make().start()
            else:
                pl.when(cond)(lambda: self.make().start())

        def wait_recv(self, cond=None):
            if cond is None:
                self.make().wait_recv()
            else:
                pl.when(cond)(lambda: self.make().wait_recv())

    def slot(g, zs):
        zs = jnp.minimum(jnp.maximum(zs, 0), Z - 1)
        if g in gather_pairs:
            return kv[g].at[pl.ds(zs * Y, Y)]
        return kv[g].at[zs * Y + y]

    def gather_up(g, k):
        item = slot(g, z - k)
        return Push(item, item, agu_s.at[g, k], agu_r.at[g, k + 1], above)

    def gather_down(g, k):
        item = slot(g, z + k)
        return Push(item, item, agd_s.at[g, k], agd_r.at[g, k + 1], below)

    def gather_across(g, k, zs):
        item = kv[g].at[jnp.minimum(jnp.maximum(zs, 0), Z - 1) * Y + y]
        return Push(item, item, agy_s.at[g, k], agy_r.at[g, k], partner)

    def gather_step(g, k):
        if k == -1:
            if Y > 1:
                gather_across(g, 0, z).start()
            return
        if k == 0:
            if g in gather_pairs and Y > 1:
                gather_across(g, 0, z).wait_recv()
            gather_up(g, 0).start(has_above)
            gather_down(g, 0).start(has_below)
            return
        up_here, down_here = z >= k, z + k < Z
        Push(slot(g, z - k), slot(g, z - k), agu_s.at[g, k], agu_r.at[g, k], me).wait_recv(up_here)
        if k < Z - 1:
            gather_up(g, k).start(up_here & has_above)
        if g not in gather_pairs and Y > 1:
            gather_across(g, k, z - k).start(up_here)
        Push(slot(g, z + k), slot(g, z + k), agd_s.at[g, k], agd_r.at[g, k], me).wait_recv(down_here)
        if k < Z - 1:
            gather_down(g, k).start(down_here & has_below)
        if g not in gather_pairs and Y > 1:
            gather_across(g, Z + k, z + k).start(down_here)

    def gather_done(g):
        if g in gather_pairs or Y == 1:
            return
        gather_across(g, 0, z).wait_recv()
        for k in range(1, Z):
            gather_across(g, k, z - k).wait_recv(z >= k)
            gather_across(g, Z + k, z + k).wait_recv(z + k < Z)

    def parent_of(a):
        return jnp.where(a >= 0, bp_ref[jnp.maximum(a, 0)], -1)

    ancestors = [bp_ref[me]]
    for l in range(1, L):
        ancestors.append(parent_of(ancestors[-1]))
    safe = [jnp.maximum(a, 0) for a in ancestors]

    def masks():
        reach = [closure_transposed(tp_ref[b]) for b in safe + [me]]
        for sweep in range((BLOCK - 1).bit_length()):
            reach = [jnp.minimum(dot(r, r, ((1,), (0,))), 1.0).astype(jnp.bfloat16) for r in reach]
        for l in range(L):
            spine = reach[l][:, BLOCK - 1:].astype(jnp.float32)
            spine = spine * jnp.where(ancestors[l] >= 0, 1.0, 0.0)
            spine = jnp.broadcast_to(spine, (BLOCK, HD))
            bias[pl.ds(l * BLOCK, BLOCK), :] = jnp.where(spine > 0.5, 0.0, MASKED)
        bias[pl.ds(L * BLOCK, BLOCK), :] = jnp.where(reach[L].astype(jnp.float32) > 0.5, 0.0, MASKED)

    def level_of(block):
        level = jnp.where(block == me, L, L + 1)
        for l in range(L):
            level = jnp.where(ancestors[l] == block, l, level)
        return level

    def compute_begin(g):
        for l in range(L):
            cur[pl.ds(l * BLOCK, BLOCK), :] = kv[g][safe[l]]
        cur[pl.ds(L * BLOCK, BLOCK), :] = kv[g][me]
        kt[...] = cur[:, :HD].T

    def compute_chunk(g, c):
        at = [pl.ds((g * R + c * CHUNK_HEADS + h) * HD, HD) for h in range(CHUNK_HEADS)]
        qc = jnp.concatenate([q_ref[:, a] for a in at], 0)
        dc = jnp.concatenate([do_ref[:, a] for a in at], 0)
        keys, values = cur[:, :HD], cur[:, HD:]
        mask = jnp.concatenate([bias[...]] * CHUNK_HEADS, 1)
        s = dot(keys, qc, ((1,), (1,))) * scale + mask
        dp = dot(values, dc, ((1,), (1,)))
        e = jnp.exp(s - jnp.max(s, 0, keepdims=True))
        inv = 1.0 / jnp.sum(e, 0, keepdims=True)
        p = e * inv
        delta = jnp.sum(p * dp, 0, keepdims=True)
        ds = (p * (dp - delta)).astype(jnp.bfloat16)
        plow = p.astype(jnp.bfloat16)
        dqt = (dot(kt[...], ds, ((1,), (0,))) * scale).T
        for h in range(CHUNK_HEADS):
            dq_ref[:, at[h]] = dqt[h * BLOCK:(h + 1) * BLOCK].astype(jnp.bfloat16)
        more_k, more_v = dot(ds, qc, ((1,), (0,))), dot(plow, dc, ((1,), (0,)))
        if c == 0:
            acc_k[...] = more_k
            acc_v[...] = more_v
        else:
            acc_k[...] += more_k
            acc_v[...] += more_v

    def compute_end(g):
        for l in range(L + 1):
            rows = pl.ds(l * BLOCK, BLOCK)
            part[g][l, :, :HD] = (acc_k[rows, :] * scale).astype(jnp.bfloat16)
            part[g][l, :, HD:] = acc_v[rows, :].astype(jnp.bfloat16)
        part[g][L + 1] = jnp.zeros((BLOCK, 2 * HD), jnp.bfloat16)

    column = [lax.rem(z + k, Z) * Y + y for k in range(Z)]

    def across(g, k):
        return Push(ysend[g].at[k], yrecv[g].at[k], rsy_s.at[g, k], rsy_r.at[g, k], partner)

    def along(g, k):
        return Push(zsend[g].at[k], zrecv[g].at[k], rsz_s.at[g, k], rsz_r.at[g, k], column[k])

    hops = list(range(1, Z)) + [0]

    def scatter_y(g):
        if Y > 1:
            for k in hops:
                ysend[g][k] = part[g][level_of(column[k] + (Y - 1 - y) - y)]
                across(g, k).start()

    def scatter_z(g):
        for k in hops:
            total = part[g][level_of(column[k])].astype(jnp.float32)
            if Y > 1:
                across(g, k).wait_recv()
                total = total + yrecv[g][k].astype(jnp.float32)
            if k == 0:
                own_sum[g] = total
            else:
                zsend[g][k] = total.astype(jnp.bfloat16)
                along(g, k).start()

    def finish(g):
        total = own_sum[g]
        for k in range(1, Z):
            along(g, k).wait_recv()
            total = total + zrecv[g][k].astype(jnp.float32)
        cols = slice(g * HD, (g + 1) * HD)
        dk_ref[:, cols] = total[:, :HD].astype(jnp.bfloat16)
        dv_ref[:, cols] = total[:, HD:].astype(jnp.bfloat16)

    for g in range(G):
        loads[2 * g].wait()
        loads[2 * g + 1].wait()
        if g < AHEAD or g in gather_pairs:
            gather_step(g, -1)
        if g < AHEAD and g not in gather_pairs:
            gather_step(g, 0)
    for copy in loads[2 * G:]:
        copy.wait()
    masks()

    steps = [(g, k) for t in range(G + Z) for g in range(G) for k in [t - g] if 0 <= k < Z]
    steps = [(g, k) for g, k in steps if k > 0 or g in gather_pairs or g >= AHEAD]
    for g in range(AHEAD, G):
        if g not in gather_pairs:
            steps.insert(steps.index((g, 0)), (g, -1))

    def gather_until(g, k):
        while steps and (g, k) in steps:
            gather_step(*steps.pop(0))

    chunks = R // CHUNK_HEADS
    for g in range(G):
        gather_until(g, Z - 1)
        gather_done(g)
        compute_begin(g)
        for c in range(chunks):
            compute_chunk(g, c)
            if g + 1 < G:
                gather_until(g + 1, (Z - 1) * (c + 1) // chunks)
        compute_end(g)
        scatter_y(g)
        if g > 0:
            scatter_z(g - 1)
    scatter_z(G - 1)
    for g in range(G):
        finish(g)
    for cond, copy in sent:
        if cond is None:
            copy.make().wait_send()
        else:
            pl.when(cond)(lambda copy=copy: copy.make().wait_send())


def on_device(queries, key_rows, value_rows, out_grad, token_parent, block_parent):
    H = lax.axis_size("hyp")
    Y = 2 if H == 8 else 1
    Z = H // Y
    L = min(5, H - 4)
    G = key_rows.shape[1] // HD
    R = queries.shape[1] // key_rows.shape[1]
    keys = (L + 1) * BLOCK
    bf, f32 = jnp.bfloat16, jnp.float32
    vmem = pl.BlockSpec(memory_space=pltpu.VMEM)
    hbm = pl.BlockSpec(memory_space=pl.ANY)
    dma = pltpu.SemaphoreType.DMA
    tile = (BLOCK, 2 * HD)
    gather_pairs = GATHER_PAIRS if Y > 1 else tuple(range(G))
    scratch = (
        [pltpu.VMEM((H,) + tile, bf)] * G
        + [pltpu.VMEM((L + 2,) + tile, bf)] * G
        + [pltpu.VMEM((Z,) + tile, bf)] * (4 * G)
        + [
            pltpu.VMEM((token_parent.shape[0] // BLOCK, 1, BLOCK), jnp.int32),
            pltpu.VMEM(queries.shape, bf),
            pltpu.VMEM(out_grad.shape, bf),
            pltpu.VMEM((keys, 2 * HD), bf),
            pltpu.VMEM((HD, keys), bf),
            pltpu.VMEM((keys, HD), f32),
            pltpu.VMEM((keys, HD), f32),
            pltpu.VMEM((keys, HD), f32),
            pltpu.VMEM((G,) + tile, f32),
            dma((2 * G + 3,)),
        ]
        + [dma((G, Z))] * 4
        + [dma((G, 2 * Z))] * 2
        + [dma((G, Z))] * 4
    )
    return pl.pallas_call(
        functools.partial(kernel, Z, Y, G, R, L, gather_pairs),
        out_shape=(
            jax.ShapeDtypeStruct(queries.shape, bf),
            jax.ShapeDtypeStruct(key_rows.shape, bf),
            jax.ShapeDtypeStruct(value_rows.shape, bf),
        ),
        in_specs=[pl.BlockSpec(memory_space=pltpu.SMEM)] + [hbm] * 5,
        out_specs=(vmem, vmem, vmem),
        scratch_shapes=scratch,
        compiler_params=pltpu.CompilerParams(
            collective_id=0, has_side_effects=True, vmem_limit_bytes=54 * 1024 * 1024),
        name="tree_attention_backward",
    )(block_parent, token_parent.reshape(-1, 1, BLOCK), queries, out_grad, key_rows, value_rows)


def solution(mesh):
    rows = P(("groups", "hyp"), "tensor")
    return jax.shard_map(
        on_device, mesh=mesh,
        in_specs=(rows, rows, rows, rows, P("groups"), P("groups")),
        out_specs=(rows, rows, rows), check_vma=False)
```
